32 devices in a mesh: date: 8 (over z, y), strip: 4 (over x, core).
Axes of the slice: x: 2, y: 2, z: 4, core: 2. Of those that a mesh axis runs over, the one named last changes fastest.
Arguments:
- scenes: bfloat16 [2, 16, 128, 4096], P(None, 'date', 'strip'), may hold values from -6 to 6
- date_pairs: int32 [12, 2], replicated, may hold values from 0 to 15, as said below
- first_weight: bfloat16 [3, 3, 64, 2], replicated, may hold values from -4 to 4
- mid_weight: bfloat16 [2, 3, 3, 64, 64], replicated, may hold values from -0.375 to 0.375
- last_weight: bfloat16 [3, 3, 1, 64], replicated, may hold values from -0.375 to 0.375
- inversion: float32 [16, 12], replicated, may hold values from -1.75 to 1.75
Outputs:
- displacement: float32 [16, 32, 256], P('date', 'strip')
The draws below stay inside these ranges and needn't reach their ends.
Inputs may be any that keep to these rules, and one draw needn't show every extreme that they name: `date_pairs`: Write g(d) = d // 2 for the date group of date d; in matching m, g of the reference date and g of the secondary date differ exactly in the bit of value step, and every group in 0..2 4 - 1 appears in exactly one interferogram of each matching. Which side is the reference and which date of a group is used vary.
All inputs are finite; a program needn't handle non-finite values.
Results may differ from the reference program's by a relative error of at most 0.02.
Values may be sent and summed in bfloat16 or wider, within the bound.
A program may use at most 64 MiB of HBM per device.

```python
import jax
import jax.numpy as jnp
import numpy as np
from jax import lax

COLS = 4096
DATE_DEV = 2
CH = 64
MIDS = 2
LOOK_R = 4
LOOK_C = 16
DEV_HALF = 4
DATES = 16
PAIRS = 12
ROWS = 128


def draw_date_pairs(key, part):
    total_groups = 2 * DEV_HALF
    bit_list = [0, 1, DEV_HALF.bit_length() - 1]
    blocks = []
    for which in range(3):
        bit_pos = bit_list[which]
        lower_groups = np.array([group for group in range(total_groups) if not group >> bit_pos & 1], np.int32)
        key_order, key_side, key_local = jax.random.split(jax.random.fold_in(key, which + 11), 3)
        shuffled = jax.random.permutation(key_order, jnp.asarray(lower_groups))
        upper_groups = shuffled + (1 << bit_pos)
        flipped = jax.random.randint(key_side, (DEV_HALF,), 0, 2)
        local_dates = jax.random.randint(key_local, (DEV_HALF, 2), 0, DATE_DEV)
        ref_group = jnp.where(flipped == 1, upper_groups, shuffled)
        sec_group = jnp.where(flipped == 1, shuffled, upper_groups)
        ref_date = ref_group * DATE_DEV + local_dates[:, 0]
        sec_date = sec_group * DATE_DEV + local_dates[:, 1]
        blocks.append(jnp.stack([ref_date, sec_date], axis=1))
    return jnp.concatenate(blocks, axis=0).astype(jnp.int32)


def block_levels(rng, dims, pieces, least, top_value):
    gain = 1.0
    for dim, parts in pieces:
        heights = jax.random.uniform(jax.random.fold_in(jax.random.fold_in(rng, 6), dim), (parts,), jnp.float32, least / len(pieces), top_value / len(pieces))
        gain = gain * jnp.repeat(jnp.exp(heights), dims[dim] // parts).reshape((-1,) + (1,) * (len(dims) - 1 - dim))
    return gain


def noise(stream_key, shape, width, bound, cuts=(), dtype=jnp.bfloat16):
    values = width * jax.random.normal(stream_key, shape, jnp.float32)
    if cuts:
        values = values * block_levels(stream_key, shape, cuts, -0.22, 0.18)
    return jnp.clip(values, -bound, bound).astype(dtype)


def setup_inputs(seed: int = 0) -> dict:
    splits = jax.random.split(jax.random.key(seed), 7)
    scenes = noise(splits[0], (2, DATES, ROWS, COLS), 1.0, 6.0, ((1, 8), (2, 4)))
    date_pairs = draw_date_pairs(jax.random.fold_in(splits[6], 71), 0)
    first_weight = noise(splits[2], (3, 3, CH, 2), 2 ** -0.5, 4.0)
    mid_weight = noise(splits[3], (MIDS, 3, 3, CH, CH), (9 * CH // 2) ** -0.5, 0.375)
    last_weight = noise(splits[4], (3, 3, 1, CH), (9 * CH // 2) ** -0.5, 0.375)
    inversion = noise(splits[5], (DATES, PAIRS), PAIRS ** -0.5, 1.75, (), jnp.float32)
    return {"scenes": scenes, "date_pairs": date_pairs, "first_weight": first_weight, "mid_weight": mid_weight, "last_weight": last_weight, "inversion": inversion}


def look_sum(field):
    lead = field.shape[:-2]
    count_rows = field.shape[-2]
    count_cols = field.shape[-1]
    shaped = field.reshape(lead + (count_rows // LOOK_R, LOOK_R, count_cols // LOOK_C, LOOK_C))
    return shaped.sum(axis=(-3, -1))

def coherence_of(first, second):
    first = first.astype(jnp.float32)
    second = second.astype(jnp.float32)
    real_part = first[0] * second[0] + first[1] * second[1]
    imag_part = first[1] * second[0] - first[0] * second[1]
    first_power = first[0] * first[0] + first[1] * first[1]
    second_power = second[0] * second[0] + second[1] * second[1]
    scale = lax.rsqrt(look_sum(first_power) * look_sum(second_power) + 1e-06)
    return (jnp.stack([look_sum(real_part), look_sum(imag_part)]) * scale).astype(jnp.bfloat16)

def convolve(field, weight):
    padded = jnp.pad(field.astype(jnp.float32), ((0, 0), (1, 1), (1, 1)))
    count_rows = field.shape[1]
    count_cols = field.shape[2]
    weight = weight.astype(jnp.float32)
    total = jnp.zeros((weight.shape[2], count_rows, count_cols), jnp.float32)
    for tap_row in range(3):
        for tap_col in range(3):
            piece = padded[:, tap_row:tap_row + count_rows, tap_col:tap_col + count_cols]
            total = total + jnp.einsum('oi,irc->orc', weight[tap_row, tap_col], piece)
    return total

def one_pair(scenes, first_weight, mid_weight, last_weight, pair_row):
    first = lax.dynamic_index_in_dim(scenes, pair_row[0], 1, keepdims=False)
    second = lax.dynamic_index_in_dim(scenes, pair_row[1], 1, keepdims=False)
    hidden = coherence_of(first, second)
    hidden = jax.nn.relu(convolve(hidden, first_weight)).astype(jnp.bfloat16)
    for inner in range(MIDS):
        hidden = jax.nn.relu(convolve(hidden, mid_weight[inner])).astype(jnp.bfloat16)
    return convolve(hidden, last_weight)[0].astype(jnp.bfloat16)

def reference(scenes, date_pairs, first_weight, mid_weight, last_weight, inversion):
    phases = lax.map(lambda pair_row: one_pair(scenes, first_weight, mid_weight, last_weight, pair_row), date_pairs)
    return jnp.einsum('dk,krc->drc', inversion, phases.astype(jnp.float32), precision=lax.Precision.HIGHEST)
```

```python
import functools

import jax
import jax.numpy as jnp
from jax import lax
from jax.experimental import pallas as pl
from jax.experimental.pallas import tpu as pltpu
from jax.sharding import PartitionSpec as P

LOOK_R = 4
LOOK_C = 16
WIN = 144
EDGE = 8
NT = (((1,), (1,)), ((), ()))
TN = (((0,), (0,)), ((), ()))
MESH = pl.DeviceIdType.MESH
F32 = jnp.float32
BF16 = jnp.bfloat16


def iota(shape, dim):
    return lax.broadcasted_iota(jnp.int32, shape, dim)


def third(value):
    return (value * 11) >> 5


def flag(cond):
    return jnp.where(cond, 1.0, 0.0)


def kernel(
    n_date,
    n_strip,
    scenes,
    pairs,
    inversion,
    w_first,
    w_mid,
    w_last,
    out,
    tile,
    sendbuf,
    recvbuf,
    select,
    prods,
    sums,
    xs,
    base_first,
    big_first,
    big_mid,
    rows_last,
    big_last,
    col_mask,
    hid_a,
    hid_b,
    hid_c,
    last_out,
    gathered,
    load_sem,
    ex_send,
    ex_recv,
    halo_send,
    halo_recv,
    ga_send,
    ga_recv,
):
    me = lax.axis_index("date")
    strip = lax.axis_index("strip")
    date_dev = scenes.shape[1]
    cols = scenes.shape[3]
    span = sendbuf.shape[-1]
    block = n_date // 2
    bits = [0, 1, n_date.bit_length() - 2]
    total_rows = n_strip * 8

    barrier = pltpu.get_barrier_semaphore()

    def greet(j, carry):
        pl.semaphore_signal(
            barrier, inc=1, device_id=(lax.rem(me + j, n_date), strip), device_id_type=MESH
        )
        return carry

    lax.fori_loop(1, n_date, greet, 0)

    @pl.when(strip > 0)
    def _():
        pl.semaphore_signal(barrier, inc=1, device_id=(me, strip - 1), device_id_type=MESH)

    @pl.when(strip < n_strip - 1)
    def _():
        pl.semaphore_signal(barrier, inc=1, device_id=(me, strip + 1), device_id_type=MESH)

    load = pltpu.make_async_copy(scenes, tile, load_sem)
    load.start()

    upper, partner, own_date, sign = [], [], [], []
    for m in range(3):
        step = 1 << bits[m]
        side = lax.rem(me // step, 2)
        upper.append(side)
        partner.append(me + step - 2 * step * side)

        def pick(i, carry, m=m):
            date, is_ref = carry
            ref = pairs[m * block + i, 0]
            sec = pairs[m * block + i, 1]
            ref_hit = ref // date_dev == me
            sec_hit = sec // date_dev == me
            date = jnp.where(ref_hit, ref, jnp.where(sec_hit, sec, date))
            return date, jnp.where(ref_hit, 1, is_ref)

        date, is_ref = lax.fori_loop(
            0, block, pick, (me * date_dev, jnp.int32(0)), unroll=block <= 8
        )
        own_date.append(date - me * date_dev)
        sign.append(jnp.where(is_ref == 1, 1.0, -1.0).astype(F32))

    load.wait()
    pl.semaphore_wait(
        barrier,
        n_date - 1 + jnp.where(strip > 0, 1, 0) + jnp.where(strip < n_strip - 1, 1, 0),
    )

    exchange = {}
    for m in (2, 0, 1):
        offset = pl.multiple_of((1 - upper[m]) * (cols - span), 128)
        for h in range(2):
            for c in range(2):
                sendbuf[m, h, c] = tile[c, own_date[m], h * 16 : h * 16 + 16, pl.ds(offset, span)]
            exchange[m, h] = pltpu.make_async_remote_copy(
                src_ref=sendbuf.at[m, h],
                dst_ref=recvbuf.at[m, h],
                send_sem=ex_send.at[m, h],
                recv_sem=ex_recv.at[m, h],
                device_id=(partner[m], strip),
                device_id_type=MESH,
            )
            exchange[m, h].start()

    def fill_select(j, carry):
        apart = iota((128, 256), 0) + j * 128 - LOOK_C * iota((128, 256), 1)
        rows = pl.ds(pl.multiple_of(j * 128, 128), 128)
        select[rows, :] = flag((apart >= 0) & (apart < LOOK_C)).astype(BF16)
        return carry

    lax.fori_loop(0, span // 128, fill_select, 0)

    base_first[...] = jnp.zeros_like(base_first)
    nothing = jnp.zeros((64, 2), BF16)
    eye_small = flag(iota((8, 2), 0) == iota((8, 2), 1)).astype(BF16)
    for b in range(4):
        for q in range(3):
            stack = jnp.concatenate(
                [w_first[b, q] if b < 3 else nothing, w_first[b - 1, q] if b > 0 else nothing],
                axis=0,
            )
            turned = lax.dot_general(eye_small, stack, NT, preferred_element_type=F32)
            place = (b * 3 + q) * 2
            base_first[place : place + 2, :] = turned[:2]
    base = base_first[...].astype(BF16)
    k = iota((96, 32), 0)
    n = iota((96, 32), 1)
    same = ((k >> 5) == (n >> 1) - 3 * third(n >> 1)) & (((k >> 2) & 1) == (n & 1))
    row = ((k >> 3) & 3) * 4 + (k & 3) - third(n >> 1)
    for i in range(7):
        pickrow = flag(same & (row == 2 * i)).astype(BF16)
        big_first[:, i * 128 : i * 128 + 128] = jnp.dot(
            pickrow, base, preferred_element_type=F32
        ).astype(BF16)

    blank = jnp.zeros((64, 64), BF16)
    eye = flag(iota((64, 64), 0) == iota((64, 64), 1)).astype(BF16)
    for layer in range(2):
        for b in range(4):
            for q in range(3):
                stack = jnp.concatenate(
                    [
                        w_mid[layer, b, q] if b < 3 else blank,
                        w_mid[layer, b - 1, q] if b > 0 else blank,
                    ],
                    axis=0,
                )
                turned = lax.dot_general(eye, stack, NT, preferred_element_type=F32)
                place = (b // 2) * 384 + q * 128 + (b % 2) * 64
                big_mid[layer, place : place + 64, :] = turned.astype(BF16)

    rows_last[...] = jnp.zeros_like(rows_last)
    for p in range(3):
        for q in range(3):
            rows_last[p * 3 + q : p * 3 + q + 1, :] = w_last[p, q].astype(F32)
    twice = flag((iota((64, 128), 1) & 63) == iota((64, 128), 0)).astype(BF16)
    both = jnp.dot(rows_last[...].astype(BF16), twice, preferred_element_type=F32).astype(BF16)
    k = iota((24, 16), 0)
    n = iota((24, 16), 1)
    same = (k >> 3) == n - 3 * third(n)
    tap = third(n) + (k & 7)
    first_half = iota((24, 128), 1) < 64
    for i in range(5):
        parts = [
            jnp.dot(
                flag(same & (tap == 2 * i + a)).astype(BF16), both, preferred_element_type=F32
            )
            for a in range(2)
        ]
        big_last[:, i * 128 : i * 128 + 128] = jnp.where(first_half, parts[0], parts[1]).astype(
            BF16
        )

    last_out[...] = jnp.zeros_like(last_out)
    window = iota((WIN, 128), 0)
    for m in range(3):
        low = EDGE * (1 - upper[m])
        col_mask[m] = flag((window >= low) & (window < WIN - EDGE + low))

    @pl.when(strip == 0)
    def _():
        xs[:, 0:8, :] = jnp.zeros((3, 8, 256), F32)

    @pl.when(strip == n_strip - 1)
    def _():
        xs[:, 24:32, :] = jnp.zeros((3, 8, 256), F32)

    def halo(m, side):
        source = 8 if side == 0 else 16
        target = 24 if side == 0 else 0
        return pltpu.make_async_remote_copy(
            src_ref=xs.at[m, source : source + 8],
            dst_ref=xs.at[m, target : target + 8],
            send_sem=halo_send.at[m, side],
            recv_sem=halo_recv.at[m, side],
            device_id=(me, strip - 1 if side == 0 else strip + 1),
            device_id_type=MESH,
        )

    def look(m, h):
        own_offset = pl.multiple_of(upper[m] * (cols - span), 128)

        def columns(start, width):
            rows = slice(h * 16, h * 16 + 16)
            own = pl.ds(pl.multiple_of(own_offset + start, 128), width)
            there = pl.ds(start, width)
            a0 = tile[0, own_date[m], rows, own].astype(F32)
            a1 = tile[1, own_date[m], rows, own].astype(F32)
            b0 = recvbuf[m, h, 0, :, there].astype(F32)
            b1 = recvbuf[m, h, 1, :, there].astype(F32)
            fields = (
                a0 * b0 + a1 * b1,
                a1 * b0 - a0 * b1,
                a0 * a0 + a1 * a1,
                b0 * b0 + b1 * b1,
            )
            for f, field in enumerate(fields):
                high = field.astype(BF16)
                prods[f * 16 : f * 16 + 16, there] = high
                prods[64 + f * 16 : 80 + f * 16, there] = (field - high.astype(F32)).astype(BF16)

        def step(j, carry):
            columns(pl.multiple_of(j * 256, 256), 256)
            return carry

        lax.fori_loop(0, span // 256, step, 0, unroll=2)
        columns(span // 256 * 256, span % 256)
        looked = jnp.dot(prods[...], select[...], preferred_element_type=F32)
        looked = looked[:64] + looked[64:]
        sums[0] = looked[:, :128]
        sums[1] = looked[:, 128:]
        halves = []
        for part in range(2):
            total = sums[part, pl.ds(0, 16, stride=4), :]
            for r in range(1, 4):
                total = total + sums[part, pl.ds(r, 16, stride=4), :]
            powers = total[8:]
            powers = powers * pltpu.roll(powers, 4, 0)
            signed = total[:8] * jnp.where(iota((8, 128), 0) < 4, 1.0, sign[m])
            halves.append((signed * lax.rsqrt(powers + 1e-06)).astype(BF16).astype(F32))
        slab = jnp.concatenate(halves, axis=1)
        slab = pltpu.roll(slab, EDGE * (1 - upper[m]), 1)
        xs[m, 8 + h * 8 : 16 + h * 8, :] = slab

        @pl.when(strip > 0 if h == 0 else strip < n_strip - 1)
        def _():
            halo(m, h).start()

    def spread(target, i, value):
        value_rows = slice(i * WIN, i * WIN + WIN)
        target[value_rows, 0:128] = pltpu.roll(value, 1, 0).astype(BF16)
        target[value_rows, 128:256] = value.astype(BF16)
        target[value_rows, 256:384] = pltpu.roll(value, WIN - 1, 0).astype(BF16)

    def masked(m, value, i, first_row):
        value = jnp.maximum(value, 0.0) * col_mask[m]
        low = first_row + 2 * i
        if low < 0 or low + 1 > 7:
            rows = strip * 8 + low + (iota((1, 128), 1) >> 6)
            value = value * flag((rows >= 0) & (rows < total_rows))
        return value

    def peer_copy(m, j):
        return pltpu.make_async_remote_copy(
            src_ref=gathered.at[m, me],
            dst_ref=gathered.at[m, me],
            send_sem=ga_send.at[m, j],
            recv_sem=ga_recv.at[m, j],
            device_id=(lax.rem(me + j, n_date), strip),
            device_id_type=MESH,
        )

    def network(m):
        @pl.when(strip > 0)
        def _():
            halo(m, 1).wait_recv()

        @pl.when(strip < n_strip - 1)
        def _():
            halo(m, 0).wait_recv()

        x = xs[m]
        x = jnp.concatenate([pltpu.roll(x, 1, 1), x, pltpu.roll(x, 255, 1)], axis=0)
        x = x.astype(BF16)
        wide = lax.dot_general(x, big_first[...], TN, preferred_element_type=F32)[:WIN]
        for i in range(7):
            spread(hid_a, i, masked(m, wide[:, i * 128 : i * 128 + 128], i, -3))
        for layer, (source, count) in enumerate(((hid_a, 6), (hid_b, 5))):
            size = count * WIN
            patches = jnp.concatenate([source[:size, :], source[WIN : WIN + size, :]], axis=1)
            wide = jnp.dot(patches, big_mid[layer], preferred_element_type=F32)
            for i in range(count):
                value = masked(m, wide[i * WIN : i * WIN + WIN], i, layer - 2)
                if layer == 0:
                    spread(hid_b, i, value)
                else:
                    hid_c[:, i * 128 : i * 128 + 128] = value.astype(BF16)
        last_out[:, :WIN] = lax.dot_general(
            big_last[...], hid_c[...], NT, preferred_element_type=F32
        )
        phase = (
            pltpu.roll(last_out[0:8], 256 - (EDGE - 1), 1)
            + pltpu.roll(last_out[8:16], 256 - EDGE, 1)
            + pltpu.roll(last_out[16:24], 256 - (EDGE + 1), 1)
        )[:, :128]
        gathered[m, me] = phase.astype(BF16).astype(F32)

        def tell(j, carry):
            peer_copy(m, j).start()
            return carry

        lax.fori_loop(1, n_date, tell, 0)

    for m in (0, 1):
        for h in range(2):
            exchange[m, h].wait_recv()
            look(m, h)
    network(0)
    network(1)
    for h in range(2):
        exchange[2, h].wait_recv()
        look(2, h)
    network(2)

    for m in range(3):
        for h in range(2):
            exchange[m, h].wait_send()

            @pl.when(strip > 0 if h == 0 else strip < n_strip - 1)
            def _(m=m, h=h):
                halo(m, h).wait_send()

        def hear(j, carry, m=m):
            copy = peer_copy(m, j)
            copy.wait_send()
            copy.wait_recv()
            return carry

        lax.fori_loop(1, n_date, hear, 0)

    zero = jnp.zeros((8, 128), F32)
    acc = (zero,) * (2 * date_dev)
    for m in range(3):

        def add(i, acc, m=m):
            pair = m * block + i
            ref = pairs[pair, 0] // date_dev
            sec = pairs[pair, 1] // date_dev
            left = gathered[m, jnp.minimum(ref, sec)]
            right = gathered[m, jnp.maximum(ref, sec)]
            result = []
            for t in range(date_dev):
                gain = inversion[me * date_dev + t, pair]
                result += [acc[2 * t] + gain * left, acc[2 * t + 1] + gain * right]
            return tuple(result)

        acc = lax.fori_loop(0, block, add, acc, unroll=block <= 8)
    for t in range(date_dev):
        out[t, :, 0:128] = acc[2 * t]
        out[t, :, 128:256] = acc[2 * t + 1]


def per_device(scenes, date_pairs, first_weight, mid_weight, last_weight, inversion):
    n_date = lax.axis_size("date")
    n_strip = lax.axis_size("strip")
    date_dev = scenes.shape[1]
    cols = scenes.shape[3]
    span = cols // 2 + EDGE * LOOK_C
    vmem = pl.BlockSpec(memory_space=pltpu.VMEM)
    smem = pl.BlockSpec(memory_space=pltpu.SMEM)
    dma = pltpu.SemaphoreType.DMA
    return pl.pallas_call(
        functools.partial(kernel, n_date, n_strip),
        out_shape=jax.ShapeDtypeStruct((date_dev, 8, 256), F32),
        in_specs=[pl.BlockSpec(memory_space=pl.ANY), smem, smem, vmem, vmem, vmem],
        out_specs=vmem,
        scratch_shapes=[
            pltpu.VMEM(scenes.shape, BF16),
            pltpu.VMEM((3, 2, 2, 16, span), BF16),
            pltpu.VMEM((3, 2, 2, 16, span), BF16),
            pltpu.VMEM((span, 256), BF16),
            pltpu.VMEM((128, span), BF16),
            pltpu.VMEM((2, 64, 128), F32),
            pltpu.VMEM((3, 32, 256), F32),
            pltpu.VMEM((32, 128), F32),
            pltpu.VMEM((96, 7 * 128), BF16),
            pltpu.VMEM((2, 768, 128), BF16),
            pltpu.VMEM((16, 64), F32),
            pltpu.VMEM((24, 5 * 128), BF16),
            pltpu.VMEM((3, WIN, 128), F32),
            pltpu.VMEM((7 * WIN, 384), BF16),
            pltpu.VMEM((6 * WIN, 384), BF16),
            pltpu.VMEM((WIN, 5 * 128), BF16),
            pltpu.VMEM((24, 256), F32),
            pltpu.VMEM((3, n_date, 8, 128), F32),
            dma,
            dma((3, 2)),
            dma((3, 2)),
            dma((3, 2)),
            dma((3, 2)),
            dma((3, n_date)),
            dma((3, n_date)),
        ],
        compiler_params=pltpu.CompilerParams(
            collective_id=0, has_side_effects=True, vmem_limit_bytes=40 * 1024 * 1024
        ),
    )(scenes, date_pairs, inversion, first_weight, mid_weight, last_weight)


def solution(mesh):
    return jax.shard_map(
        per_device,
        mesh=mesh,
        in_specs=(P(None, "date", "strip", None), P(), P(), P(), P(), P()),
        out_specs=P("date", "strip", None),
        check_vma=False,
    )
```

```python
import functools

import jax
import jax.numpy as jnp
from jax import lax
from jax.experimental import pallas as pl
from jax.experimental.pallas import tpu as pltpu
from jax.sharding import PartitionSpec as P

LOOK_R = 4
LOOK_C = 16
WIN = 144
EDGE = 8
NT = (((1,), (1,)), ((), ()))
TN = (((0,), (0,)), ((), ()))
MESH = pl.DeviceIdType.MESH
F32 = jnp.float32
BF16 = jnp.bfloat16


def iota(shape, dim):
    return lax.broadcasted_iota(jnp.int32, shape, dim)


def third(value):
    return (value * 11) >> 5


def flag(cond):
    return jnp.where(cond, 1.0, 0.0)


def kernel(
    n_date,
    n_strip,
    scenes,
    pairs_hbm,
    inversion_hbm,
    w_first_hbm,
    w_mid_hbm,
    w_last_hbm,
    out,
    pairs,
    inversion,
    w_first,
    w_mid,
    w_last,
    tile,
    sendbuf,
    recvbuf,
    select,
    prods,
    sums,
    xs,
    base_first,
    big_first,
    big_mid,
    rows_last,
    big_last,
    col_mask,
    hid_a,
    hid_b,
    hid_c,
    last_out,
    gathered,
    load_sem,
    ex_send,
    ex_recv,
    halo_send,
    halo_recv,
    ga_send,
    ga_recv,
):
    me = lax.axis_index("date")
    strip = lax.axis_index("strip")
    date_dev = scenes.shape[1]
    cols = scenes.shape[3]
    span = sendbuf.shape[-1]
    block = n_date // 2
    bits = [0, 1, n_date.bit_length() - 2]
    total_rows = n_strip * 8

    barrier = pltpu.get_barrier_semaphore()

    def greet(j, carry):
        pl.semaphore_signal(
            barrier, inc=1, device_id=(lax.rem(me + j, n_date), strip), device_id_type=MESH
        )
        return carry

    lax.fori_loop(1, n_date, greet, 0)

    @pl.when(strip > 0)
    def _():
        pl.semaphore_signal(barrier, inc=1, device_id=(me, strip - 1), device_id_type=MESH)

    @pl.when(strip < n_strip - 1)
    def _():
        pl.semaphore_signal(barrier, inc=1, device_id=(me, strip + 1), device_id_type=MESH)

    loads = [
        pltpu.make_async_copy(source, target, load_sem.at[i])
        for i, (source, target) in enumerate(
            (
                (pairs_hbm, pairs),
                (scenes, tile),
                (w_first_hbm, w_first),
                (w_mid_hbm, w_mid),
                (w_last_hbm, w_last),
                (inversion_hbm, inversion),
            )
        )
    ]
    for load in loads:
        load.start()
    loads[0].wait()

    upper, partner, own_date, sign = [], [], [], []
    for m in range(3):
        step = 1 << bits[m]
        side = lax.rem(me // step, 2)
        upper.append(side)
        partner.append(me + step - 2 * step * side)

        def pick(i, carry, m=m):
            date, is_ref = carry
            ref = pairs[0, m * block + i]
            sec = pairs[1, m * block + i]
            ref_hit = ref // date_dev == me
            sec_hit = sec // date_dev == me
            date = jnp.where(ref_hit, ref, jnp.where(sec_hit, sec, date))
            return date, jnp.where(ref_hit, 1, is_ref)

        date, is_ref = lax.fori_loop(
            0, block, pick, (me * date_dev, jnp.int32(0)), unroll=block <= 8
        )
        own_date.append(date - me * date_dev)
        sign.append(jnp.where(is_ref == 1, 1.0, -1.0).astype(F32))

    loads[1].wait()
    pl.semaphore_wait(
        barrier,
        n_date - 1 + jnp.where(strip > 0, 1, 0) + jnp.where(strip < n_strip - 1, 1, 0),
    )

    exchange = {}
    for m in (2, 0, 1):
        offset = pl.multiple_of((1 - upper[m]) * (cols - span), 128)
        for h in range(2):
            for c in range(2):
                sendbuf[m, h, c] = tile[c, own_date[m], h * 16 : h * 16 + 16, pl.ds(offset, span)]
            exchange[m, h] = pltpu.make_async_remote_copy(
                src_ref=sendbuf.at[m, h],
                dst_ref=recvbuf.at[m, h],
                send_sem=ex_send.at[m, h],
                recv_sem=ex_recv.at[m, h],
                device_id=(partner[m], strip),
                device_id_type=MESH,
            )
            exchange[m, h].start()

    def fill_select(j, carry):
        apart = iota((128, 256), 0) + j * 128 - LOOK_C * iota((128, 256), 1)
        rows = pl.ds(pl.multiple_of(j * 128, 128), 128)
        select[rows, :] = flag((apart >= 0) & (apart < LOOK_C)).astype(BF16)
        return carry

    lax.fori_loop(0, span // 128, fill_select, 0)

    for load in loads[2:]:
        load.wait()
    base_first[...] = jnp.zeros_like(base_first)
    for b in range(4):
        for q in range(3):
            place = (b * 3 + q) * 2
            if b < 3:
                base_first[place : place + 2, 0:64] = w_first[b, q].astype(F32)
            if b > 0:
                base_first[place : place + 2, 64:128] = w_first[b - 1, q].astype(F32)
    base = base_first[...].astype(BF16)
    k = iota((96, 32), 0)
    n = iota((96, 32), 1)
    same = ((k >> 5) == (n >> 1) - 3 * third(n >> 1)) & (((k >> 2) & 1) == (n & 1))
    row = ((k >> 3) & 3) * 4 + (k & 3) - third(n >> 1)
    for i in range(7):
        pickrow = flag(same & (row == 2 * i)).astype(BF16)
        big_first[:, i * 128 : i * 128 + 128] = jnp.dot(
            pickrow, base, preferred_element_type=F32
        ).astype(BF16)

    blank = jnp.zeros((64, 64), BF16)
    eye = flag(iota((64, 64), 0) == iota((64, 64), 1)).astype(BF16)
    for layer in range(2):
        for b in range(4):
            for q in range(3):
                stack = jnp.concatenate(
                    [
                        w_mid[layer, b, q] if b < 3 else blank,
                        w_mid[layer, b - 1, q] if b > 0 else blank,
                    ],
                    axis=0,
                )
                turned = lax.dot_general(eye, stack, NT, preferred_element_type=F32)
                place = (b // 2) * 384 + q * 128 + (b % 2) * 64
                big_mid[layer, place : place + 64, :] = turned.astype(BF16)

    rows_last[...] = jnp.zeros_like(rows_last)
    for p in range(3):
        rows_last[p * 3 : p * 3 + 3, :] = w_last[p, 0].astype(F32)
    twice = flag((iota((64, 128), 1) & 63) == iota((64, 128), 0)).astype(BF16)
    both = jnp.dot(rows_last[...].astype(BF16), twice, preferred_element_type=F32).astype(BF16)
    k = iota((24, 16), 0)
    n = iota((24, 16), 1)
    same = (k >> 3) == n - 3 * third(n)
    tap = third(n) + (k & 7)
    first_half = iota((24, 128), 1) < 64
    for i in range(5):
        parts = [
            jnp.dot(
                flag(same & (tap == 2 * i + a)).astype(BF16), both, preferred_element_type=F32
            )
            for a in range(2)
        ]
        big_last[:, i * 128 : i * 128 + 128] = jnp.where(first_half, parts[0], parts[1]).astype(
            BF16
        )

    last_out[...] = jnp.zeros_like(last_out)
    window = iota((WIN, 128), 0)
    for m in range(3):
        low = EDGE * (1 - upper[m])
        col_mask[m] = flag((window >= low) & (window < WIN - EDGE + low))

    @pl.when(strip == 0)
    def _():
        xs[:, 0:8, :] = jnp.zeros((3, 8, 256), F32)

    @pl.when(strip == n_strip - 1)
    def _():
        xs[:, 24:32, :] = jnp.zeros((3, 8, 256), F32)

    def halo(m, side):
        source = 8 if side == 0 else 16
        target = 24 if side == 0 else 0
        return pltpu.make_async_remote_copy(
            src_ref=xs.at[m, source : source + 8],
            dst_ref=xs.at[m, target : target + 8],
            send_sem=halo_send.at[m, side],
            recv_sem=halo_recv.at[m, side],
            device_id=(me, strip - 1 if side == 0 else strip + 1),
            device_id_type=MESH,
        )

    def look(m, h):
        own_offset = pl.multiple_of(upper[m] * (cols - span), 128)

        def columns(start, width):
            rows = slice(h * 16, h * 16 + 16)
            own = pl.ds(pl.multiple_of(own_offset + start, 128), width)
            there = pl.ds(start, width)
            a0 = tile[0, own_date[m], rows, own].astype(F32)
            a1 = tile[1, own_date[m], rows, own].astype(F32)
            b0 = recvbuf[m, h, 0, :, there].astype(F32)
            b1 = recvbuf[m, h, 1, :, there].astype(F32)
            fields = (
                a0 * b0 + a1 * b1,
                a1 * b0 - a0 * b1,
                a0 * a0 + a1 * a1,
                b0 * b0 + b1 * b1,
            )
            for f, field in enumerate(fields):
                high = field.astype(BF16)
                prods[f * 16 : f * 16 + 16, there] = high
                prods[64 + f * 16 : 80 + f * 16, there] = (field - high.astype(F32)).astype(BF16)

        def step(j, carry):
            columns(pl.multiple_of(j * 256, 256), 256)
            return carry

        lax.fori_loop(0, span // 256, step, 0, unroll=2)
        columns(span // 256 * 256, span % 256)
        looked = jnp.dot(prods[...], select[...], preferred_element_type=F32)
        looked = looked[:64] + looked[64:]
        sums[0] = looked[:, :128]
        sums[1] = looked[:, 128:]
        halves = []
        for part in range(2):
            total = sums[part, pl.ds(0, 16, stride=4), :]
            for r in range(1, 4):
                total = total + sums[part, pl.ds(r, 16, stride=4), :]
            powers = total[8:]
            powers = powers * pltpu.roll(powers, 4, 0)
            signed = total[:8] * jnp.where(iota((8, 128), 0) < 4, 1.0, sign[m])
            halves.append((signed * lax.rsqrt(powers + 1e-06)).astype(BF16).astype(F32))
        slab = jnp.concatenate(halves, axis=1)
        slab = pltpu.roll(slab, EDGE * (1 - upper[m]), 1)
        xs[m, 8 + h * 8 : 16 + h * 8, :] = slab

        @pl.when(strip > 0 if h == 0 else strip < n_strip - 1)
        def _():
            halo(m, h).start()

    def spread(target, i, value):
        value_rows = slice(i * WIN, i * WIN + WIN)
        target[value_rows, 0:128] = pltpu.roll(value, 1, 0).astype(BF16)
        target[value_rows, 128:256] = value.astype(BF16)
        target[value_rows, 256:384] = pltpu.roll(value, WIN - 1, 0).astype(BF16)

    def masked(m, value, i, first_row):
        value = jnp.maximum(value, 0.0) * col_mask[m]
        low = first_row + 2 * i
        if low < 0 or low + 1 > 7:
            rows = strip * 8 + low + (iota((1, 128), 1) >> 6)
            value = value * flag((rows >= 0) & (rows < total_rows))
        return value

    def peer_copy(m, j):
        return pltpu.make_async_remote_copy(
            src_ref=gathered.at[m, me],
            dst_ref=gathered.at[m, me],
            send_sem=ga_send.at[m, j],
            recv_sem=ga_recv.at[m, j],
            device_id=(lax.rem(me + j, n_date), strip),
            device_id_type=MESH,
        )

    def network(m):
        @pl.when(strip > 0)
        def _():
            halo(m, 1).wait_recv()

        @pl.when(strip < n_strip - 1)
        def _():
            halo(m, 0).wait_recv()

        x = xs[m]
        x = jnp.concatenate([pltpu.roll(x, 1, 1), x, pltpu.roll(x, 255, 1)], axis=0)
        x = x.astype(BF16)
        wide = lax.dot_general(x, big_first[...], TN, preferred_element_type=F32)[:WIN]
        for i in range(7):
            spread(hid_a, i, masked(m, wide[:, i * 128 : i * 128 + 128], i, -3))
        for layer, (source, count) in enumerate(((hid_a, 6), (hid_b, 5))):
            size = count * WIN
            patches = jnp.concatenate([source[:size, :], source[WIN : WIN + size, :]], axis=1)
            wide = jnp.dot(patches, big_mid[layer], preferred_element_type=F32)
            for i in range(count):
                value = masked(m, wide[i * WIN : i * WIN + WIN], i, layer - 2)
                if layer == 0:
                    spread(hid_b, i, value)
                else:
                    hid_c[:, i * 128 : i * 128 + 128] = value.astype(BF16)
        last_out[:, :WIN] = lax.dot_general(
            big_last[...], hid_c[...], NT, preferred_element_type=F32
        )
        phase = (
            pltpu.roll(last_out[0:8], 256 - (EDGE - 1), 1)
            + pltpu.roll(last_out[8:16], 256 - EDGE, 1)
            + pltpu.roll(last_out[16:24], 256 - (EDGE + 1), 1)
        )[:, :128]
        gathered[m, me] = phase.astype(BF16).astype(F32)

        def tell(j, carry):
            peer_copy(m, j).start()
            return carry

        lax.fori_loop(1, n_date, tell, 0)

    for m in (0, 1):
        for h in range(2):
            exchange[m, h].wait_recv()
            look(m, h)
    network(0)
    network(1)
    for h in range(2):
        exchange[2, h].wait_recv()
        look(2, h)
    network(2)

    for m in range(3):
        for h in range(2):
            exchange[m, h].wait_send()

            @pl.when(strip > 0 if h == 0 else strip < n_strip - 1)
            def _(m=m, h=h):
                halo(m, h).wait_send()

        def hear(j, carry, m=m):
            copy = peer_copy(m, j)
            copy.wait_send()
            copy.wait_recv()
            return carry

        lax.fori_loop(1, n_date, hear, 0)

    zero = jnp.zeros((8, 128), F32)
    acc = (zero,) * (2 * date_dev)
    for m in range(3):

        def add(i, acc, m=m):
            pair = m * block + i
            ref = pairs[0, pair] // date_dev
            sec = pairs[1, pair] // date_dev
            left = gathered[m, jnp.minimum(ref, sec)]
            right = gathered[m, jnp.maximum(ref, sec)]
            result = []
            for t in range(date_dev):
                gain = inversion[me * date_dev + t, pair]
                result += [acc[2 * t] + gain * left, acc[2 * t + 1] + gain * right]
            return tuple(result)

        acc = lax.fori_loop(0, block, add, acc, unroll=block <= 8)
    for t in range(date_dev):
        out[t, :, 0:128] = acc[2 * t]
        out[t, :, 128:256] = acc[2 * t + 1]


def per_device(scenes, date_pairs, first_weight, mid_weight, last_weight, inversion):
    n_date = lax.axis_size("date")
    n_strip = lax.axis_size("strip")
    date_dev = scenes.shape[1]
    cols = scenes.shape[3]
    span = cols // 2 + EDGE * LOOK_C
    vmem = pl.BlockSpec(memory_space=pltpu.VMEM)
    operands = (
        scenes,
        date_pairs.T,
        inversion,
        first_weight.transpose(0, 1, 3, 2),
        mid_weight,
        last_weight.transpose(0, 2, 1, 3),
    )
    dma = pltpu.SemaphoreType.DMA
    return pl.pallas_call(
        functools.partial(kernel, n_date, n_strip),
        out_shape=jax.ShapeDtypeStruct((date_dev, 8, 256), F32),
        in_specs=[pl.BlockSpec(memory_space=pl.ANY)] * 6,
        out_specs=vmem,
        scratch_shapes=[
            pltpu.SMEM(operands[1].shape, jnp.int32),
            pltpu.SMEM(operands[2].shape, F32),
            pltpu.VMEM(operands[3].shape, BF16),
            pltpu.VMEM(operands[4].shape, BF16),
            pltpu.VMEM(operands[5].shape, BF16),
            pltpu.VMEM(scenes.shape, BF16),
            pltpu.VMEM((3, 2, 2, 16, span), BF16),
            pltpu.VMEM((3, 2, 2, 16, span), BF16),
            pltpu.VMEM((span, 256), BF16),
            pltpu.VMEM((128, span), BF16),
            pltpu.VMEM((2, 64, 128), F32),
            pltpu.VMEM((3, 32, 256), F32),
            pltpu.VMEM((32, 128), F32),
            pltpu.VMEM((96, 7 * 128), BF16),
            pltpu.VMEM((2, 768, 128), BF16),
            pltpu.VMEM((16, 64), F32),
            pltpu.VMEM((24, 5 * 128), BF16),
            pltpu.VMEM((3, WIN, 128), F32),
            pltpu.VMEM((7 * WIN, 384), BF16),
            pltpu.VMEM((6 * WIN, 384), BF16),
            pltpu.VMEM((WIN, 5 * 128), BF16),
            pltpu.VMEM((24, 256), F32),
            pltpu.VMEM((3, n_date, 8, 128), F32),
            dma((6,)),
            dma((3, 2)),
            dma((3, 2)),
            dma((3, 2)),
            dma((3, 2)),
            dma((3, n_date)),
            dma((3, n_date)),
        ],
        compiler_params=pltpu.CompilerParams(
            collective_id=0, has_side_effects=True, vmem_limit_bytes=60 * 1024 * 1024
        ),
    )(*operands)


def solution(mesh):
    return jax.shard_map(
        per_device,
        mesh=mesh,
        in_specs=(P(None, "date", "strip", None), P(), P(), P(), P(), P()),
        out_specs=P("date", "strip", None),
        check_vma=False,
    )
```

```python
import functools

import jax
import jax.numpy as jnp
from jax import lax
from jax.experimental import pallas as pl
from jax.experimental.pallas import tpu as pltpu
from jax.sharding import PartitionSpec as P

LOOK_R = 4
LOOK_C = 16
WIN = 144
EDGE = 8
NT = (((1,), (1,)), ((), ()))
TN = (((0,), (0,)), ((), ()))
MESH = pl.DeviceIdType.MESH
F32 = jnp.float32
BF16 = jnp.bfloat16


def iota(shape, dim):
    return lax.broadcasted_iota(jnp.int32, shape, dim)


def third(value):
    return (value * 11) >> 5


def flag(cond):
    return jnp.where(cond, 1.0, 0.0)


def kernel(
    n_date,
    n_strip,
    scenes,
    pairs_hbm,
    inversion_hbm,
    w_first_hbm,
    w_mid_hbm,
    w_last_hbm,
    out,
    pairs,
    inversion,
    w_first,
    w_mid,
    w_last,
    tile_0,
    tile_1,
    sendbuf,
    recvbuf,
    select,
    prods,
    sums,
    xs,
    base_first,
    big_first,
    big_mid,
    rows_last,
    big_last,
    col_mask,
    hid_a,
    hid_b,
    hid_c,
    last_out,
    gathered_0,
    gathered_1,
    gathered_2,
    ready,
    load_sem,
    tile_sem,
    ex_send,
    ex_recv,
    halo_send,
    halo_recv,
    ga_send,
    ga_recv,
):
    me = lax.axis_index("date")
    strip = lax.axis_index("strip")
    date_dev = scenes.shape[1]
    cols = scenes.shape[3]
    span = sendbuf.shape[-1]
    block = n_date // 2
    bits = [0, 1, n_date.bit_length() - 2]
    total_rows = n_strip * 8

    tile = (tile_0, tile_1)
    gathered = (gathered_0, gathered_1, gathered_2)

    barrier = pltpu.get_barrier_semaphore()

    relayed = n_date == 8
    if relayed:
        greeted = 3
        for bit in bits:
            step = 1 << bit
            other = me + step - 2 * step * lax.rem(me // step, 2)
            pl.semaphore_signal(barrier, inc=1, device_id=(other, strip), device_id_type=MESH)
    else:
        greeted = n_date - 1

        def greet(j, carry):
            pl.semaphore_signal(
                barrier, inc=1, device_id=(lax.rem(me + j, n_date), strip), device_id_type=MESH
            )
            return carry

        lax.fori_loop(1, n_date, greet, 0)

    @pl.when(strip > 0)
    def _():
        pl.semaphore_signal(barrier, inc=1, device_id=(me, strip - 1), device_id_type=MESH)

    @pl.when(strip < n_strip - 1)
    def _():
        pl.semaphore_signal(barrier, inc=1, device_id=(me, strip + 1), device_id_type=MESH)

    loads = [
        pltpu.make_async_copy(source, target, load_sem.at[i])
        for i, (source, target) in enumerate(
            (
                (pairs_hbm, pairs),
                (w_first_hbm, w_first),
                (w_mid_hbm, w_mid),
                (w_last_hbm, w_last),
                (inversion_hbm, inversion),
            )
        )
    ]
    tile_loads = [
        pltpu.make_async_copy(
            scenes.at[c, :, h * 16 : h * 16 + 16],
            tile[h].at[c],
            tile_sem.at[c, h],
        )
        for h in range(2)
        for c in range(2)
    ]
    loads[0].start()
    for load in tile_loads + loads[1:]:
        load.start()
    loads[0].wait()

    upper, partner, own_date, sign = [], [], [], []
    for m in range(3):
        step = 1 << bits[m]
        side = lax.rem(me // step, 2)
        upper.append(side)
        partner.append(me + step - 2 * step * side)

        def pick(i, carry, m=m):
            date, is_ref = carry
            ref = pairs[0, m * block + i]
            sec = pairs[1, m * block + i]
            ref_hit = ref // date_dev == me
            sec_hit = sec // date_dev == me
            date = jnp.where(ref_hit, ref, jnp.where(sec_hit, sec, date))
            return date, jnp.where(ref_hit, 1, is_ref)

        date, is_ref = lax.fori_loop(
            0, block, pick, (me * date_dev, jnp.int32(0)), unroll=block <= 8
        )
        own_date.append(date - me * date_dev)
        sign.append(jnp.where(is_ref == 1, 1.0, -1.0).astype(F32))

    exchange = {}
    for h in range(2):
        for load in tile_loads[2 * h : 2 * h + 2]:
            load.wait()
        for m in range(3):
            offset = pl.multiple_of((1 - upper[m]) * (cols - span), 128)
            for c in range(2):
                sendbuf[m, h, c] = tile[h][c, own_date[m], :, pl.ds(offset, span)]
            exchange[m, h] = pltpu.make_async_remote_copy(
                src_ref=sendbuf.at[m, h],
                dst_ref=recvbuf.at[m, h],
                send_sem=ex_send.at[m, h],
                recv_sem=ex_recv.at[m, h],
                device_id=(partner[m], strip),
                device_id_type=MESH,
            )
        if h == 0:
            pl.semaphore_wait(
                barrier,
                greeted + jnp.where(strip > 0, 1, 0) + jnp.where(strip < n_strip - 1, 1, 0),
            )
            for m in (2, 0, 1):
                exchange[m, h].start()

    def fill_select(j, carry):
        apart = iota((128, 256), 0) + j * 128 - LOOK_C * iota((128, 256), 1)
        rows = pl.ds(pl.multiple_of(j * 128, 128), 128)
        select[rows, :] = flag((apart >= 0) & (apart < LOOK_C)).astype(BF16)
        return carry

    lax.fori_loop(0, span // 128, fill_select, 0)

    for load in loads[1:]:
        load.wait()
    base_first[...] = jnp.zeros_like(base_first)
    for b in range(4):
        for q in range(3):
            place = (b * 3 + q) * 2
            if b < 3:
                base_first[place : place + 2, 0:64] = w_first[b, q].astype(F32)
            if b > 0:
                base_first[place : place + 2, 64:128] = w_first[b - 1, q].astype(F32)
    base = base_first[...].astype(BF16)
    k = iota((96, 32), 0)
    n = iota((96, 32), 1)
    same = ((k >> 5) == (n >> 1) - 3 * third(n >> 1)) & (((k >> 2) & 1) == (n & 1))
    row = ((k >> 3) & 3) * 4 + (k & 3) - third(n >> 1)
    for i in range(7):
        pickrow = flag(same & (row == 2 * i)).astype(BF16)
        big_first[:, i * 128 : i * 128 + 128] = jnp.dot(
            pickrow, base, preferred_element_type=F32
        ).astype(BF16)

    blank = jnp.zeros((64, 64), BF16)
    eye = flag(iota((64, 64), 0) == iota((64, 64), 1)).astype(BF16)
    for layer in range(2):
        for b in range(4):
            for q in range(3):
                stack = jnp.concatenate(
                    [
                        w_mid[layer, b, q] if b < 3 else blank,
                        w_mid[layer, b - 1, q] if b > 0 else blank,
                    ],
                    axis=0,
                )
                turned = lax.dot_general(eye, stack, NT, preferred_element_type=F32)
                place = (b // 2) * 384 + q * 128 + (b % 2) * 64
                big_mid[layer, place : place + 64, :] = turned.astype(BF16)

    rows_last[...] = jnp.zeros_like(rows_last)
    for p in range(3):
        rows_last[p * 3 : p * 3 + 3, :] = w_last[p, 0].astype(F32)
    twice = flag((iota((64, 128), 1) & 63) == iota((64, 128), 0)).astype(BF16)
    both = jnp.dot(rows_last[...].astype(BF16), twice, preferred_element_type=F32).astype(BF16)
    k = iota((24, 16), 0)
    n = iota((24, 16), 1)
    same = (k >> 3) == n - 3 * third(n)
    tap = third(n) + (k & 7)
    first_half = iota((24, 128), 1) < 64
    for i in range(5):
        parts = [
            jnp.dot(
                flag(same & (tap == 2 * i + a)).astype(BF16), both, preferred_element_type=F32
            )
            for a in range(2)
        ]
        big_last[:, i * 128 : i * 128 + 128] = jnp.where(first_half, parts[0], parts[1]).astype(
            BF16
        )

    last_out[...] = jnp.zeros_like(last_out)
    window = iota((WIN, 128), 0)
    for m in range(3):
        low = EDGE * (1 - upper[m])
        col_mask[m] = flag((window >= low) & (window < WIN - EDGE + low))

    @pl.when(strip == 0)
    def _():
        xs[:, 0:8, :] = jnp.zeros((3, 8, 256), F32)

    @pl.when(strip == n_strip - 1)
    def _():
        xs[:, 24:32, :] = jnp.zeros((3, 8, 256), F32)

    def halo(m, side):
        source = 8 if side == 0 else 16
        target = 24 if side == 0 else 0
        return pltpu.make_async_remote_copy(
            src_ref=xs.at[m, source : source + 8],
            dst_ref=xs.at[m, target : target + 8],
            send_sem=halo_send.at[m, side],
            recv_sem=halo_recv.at[m, side],
            device_id=(me, strip - 1 if side == 0 else strip + 1),
            device_id_type=MESH,
        )

    def look(m, h):
        own_offset = pl.multiple_of(upper[m] * (cols - span), 128)

        def columns(start, width):
            own = pl.ds(pl.multiple_of(own_offset + start, 128), width)
            there = pl.ds(start, width)
            a0 = tile[h][0, own_date[m], :, own].astype(F32)
            a1 = tile[h][1, own_date[m], :, own].astype(F32)
            b0 = recvbuf[m, h, 0, :, there].astype(F32)
            b1 = recvbuf[m, h, 1, :, there].astype(F32)
            fields = (
                a0 * b0 + a1 * b1,
                a1 * b0 - a0 * b1,
                a0 * a0 + a1 * a1,
                b0 * b0 + b1 * b1,
            )
            for f, field in enumerate(fields):
                high = field.astype(BF16)
                prods[f * 16 : f * 16 + 16, there] = high
                prods[64 + f * 16 : 80 + f * 16, there] = (field - high.astype(F32)).astype(BF16)

        def step(j, carry):
            columns(pl.multiple_of(j * 256, 256), 256)
            return carry

        lax.fori_loop(0, span // 256, step, 0, unroll=2)
        columns(span // 256 * 256, span % 256)
        looked = jnp.dot(prods[...], select[...], preferred_element_type=F32)
        looked = looked[:64] + looked[64:]
        sums[0] = looked[:, :128]
        sums[1] = looked[:, 128:]
        halves = []
        for part in range(2):
            total = sums[part, pl.ds(0, 16, stride=4), :]
            for r in range(1, 4):
                total = total + sums[part, pl.ds(r, 16, stride=4), :]
            powers = total[8:]
            powers = powers * pltpu.roll(powers, 4, 0)
            signed = total[:8] * jnp.where(iota((8, 128), 0) < 4, 1.0, sign[m])
            halves.append((signed * lax.rsqrt(powers + 1e-06)).astype(BF16).astype(F32))
        slab = jnp.concatenate(halves, axis=1)
        slab = pltpu.roll(slab, EDGE * (1 - upper[m]), 1)
        xs[m, 8 + h * 8 : 16 + h * 8, :] = slab

        @pl.when(strip > 0 if h == 0 else strip < n_strip - 1)
        def _():
            halo(m, h).start()

    def spread(target, i, value):
        value_rows = slice(i * WIN, i * WIN + WIN)
        target[value_rows, 0:128] = pltpu.roll(value, 1, 0).astype(BF16)
        target[value_rows, 128:256] = value.astype(BF16)
        target[value_rows, 256:384] = pltpu.roll(value, WIN - 1, 0).astype(BF16)

    def masked(m, value, i, first_row):
        value = jnp.maximum(value, 0.0) * col_mask[m]
        low = first_row + 2 * i
        if low < 0 or low + 1 > 7:
            rows = strip * 8 + low + (iota((1, 128), 1) >> 6)
            value = value * flag((rows >= 0) & (rows < total_rows))
        return value

    def peer_copy(m, j):
        return pltpu.make_async_remote_copy(
            src_ref=gathered[m].at[me],
            dst_ref=gathered[m].at[me],
            send_sem=ga_send.at[m, j],
            recv_sem=ga_recv.at[m, j],
            device_id=(lax.rem(me + j, n_date), strip),
            device_id_type=MESH,
        )

    def network(m):
        @pl.when(strip > 0)
        def _():
            halo(m, 1).wait_recv()

        @pl.when(strip < n_strip - 1)
        def _():
            halo(m, 0).wait_recv()

        x = xs[m]
        x = jnp.concatenate([pltpu.roll(x, 1, 1), x, pltpu.roll(x, 255, 1)], axis=0)
        x = x[:, :WIN].astype(BF16)
        wide = lax.dot_general(x, big_first[...], TN, preferred_element_type=F32)
        for i in range(7):
            spread(hid_a, i, masked(m, wide[:, i * 128 : i * 128 + 128], i, -3))
        for layer, (source, count) in enumerate(((hid_a, 6), (hid_b, 5))):
            size = count * WIN
            patches = jnp.concatenate([source[:size, :], source[WIN : WIN + size, :]], axis=1)
            wide = jnp.dot(patches, big_mid[layer], preferred_element_type=F32)
            for i in range(count):
                value = masked(m, wide[i * WIN : i * WIN + WIN], i, layer - 2)
                if layer == 0:
                    spread(hid_b, i, value)
                else:
                    hid_c[:, i * 128 : i * 128 + 128] = value.astype(BF16)
        last_out[:, :WIN] = lax.dot_general(
            big_last[...], hid_c[...], NT, preferred_element_type=F32
        )
        phase = (
            pltpu.roll(last_out[0:8], 256 - (EDGE - 1), 1)
            + pltpu.roll(last_out[8:16], 256 - EDGE, 1)
            + pltpu.roll(last_out[16:24], 256 - (EDGE + 1), 1)
        )[:, :128]
        gathered[m][me] = phase.astype(BF16).astype(F32)

        def tell(j, carry):
            peer_copy(m, j).start()
            return carry

        lax.fori_loop(1, n_date, tell, 0)

    exchange[0, 0].wait_send()
    for m in (2, 0, 1):
        exchange[m, 1].start()
    for h, m in ((0, 0), (0, 1), (1, 0), (1, 1)):
        exchange[m, h].wait_recv()
        if relayed and (m, h) == (1, 0):
            pl.semaphore_signal(ready, inc=1, device_id=(partner[0], strip), device_id_type=MESH)
        look(m, h)
    if relayed:
        pl.semaphore_wait(ready, 1)
    network(0)
    for h in range(2):
        exchange[2, h].wait_recv()
        look(2, h)
    network(1)
    network(2)

    zero = jnp.zeros((8, 128), F32)
    acc = (zero,) * (2 * date_dev)
    for m in range(3):

        def hear(j, carry, m=m):
            peer_copy(m, j).wait_recv()
            return carry

        lax.fori_loop(1, n_date, hear, 0)

        def add(i, acc, m=m):
            pair = m * block + i
            ref = pairs[0, pair] // date_dev
            sec = pairs[1, pair] // date_dev
            left = gathered[m][jnp.minimum(ref, sec)]
            right = gathered[m][jnp.maximum(ref, sec)]
            result = []
            for t in range(date_dev):
                gain = inversion[me * date_dev + t, pair]
                result += [acc[2 * t] + gain * left, acc[2 * t + 1] + gain * right]
            return tuple(result)

        acc = lax.fori_loop(0, block, add, acc, unroll=block <= 8)
    for t in range(date_dev):
        out[t, :, 0:128] = acc[2 * t]
        out[t, :, 128:256] = acc[2 * t + 1]

    for m in range(3):
        for h in range(2):
            if (m, h) != (0, 0):
                exchange[m, h].wait_send()

            @pl.when(strip > 0 if h == 0 else strip < n_strip - 1)
            def _(m=m, h=h):
                halo(m, h).wait_send()

        def sent(j, carry, m=m):
            peer_copy(m, j).wait_send()
            return carry

        lax.fori_loop(1, n_date, sent, 0)


def per_device(scenes, date_pairs, first_weight, mid_weight, last_weight, inversion):
    n_date = lax.axis_size("date")
    n_strip = lax.axis_size("strip")
    date_dev = scenes.shape[1]
    cols = scenes.shape[3]
    span = cols // 2 + EDGE * LOOK_C
    vmem = pl.BlockSpec(memory_space=pltpu.VMEM)
    operands = (
        scenes,
        date_pairs.T,
        inversion,
        first_weight.transpose(0, 1, 3, 2),
        mid_weight,
        last_weight.transpose(0, 2, 1, 3),
    )
    dma = pltpu.SemaphoreType.DMA
    return pl.pallas_call(
        functools.partial(kernel, n_date, n_strip),
        out_shape=jax.ShapeDtypeStruct((date_dev, 8, 256), F32),
        in_specs=[pl.BlockSpec(memory_space=pl.ANY)] * 6,
        out_specs=vmem,
        scratch_shapes=[
            pltpu.SMEM(operands[1].shape, jnp.int32),
            pltpu.SMEM(operands[2].shape, F32),
            pltpu.VMEM(operands[3].shape, BF16),
            pltpu.VMEM(operands[4].shape, BF16),
            pltpu.VMEM(operands[5].shape, BF16),
            *(pltpu.VMEM((2, date_dev, 16, cols), BF16),) * 2,
            pltpu.VMEM((3, 2, 2, 16, span), BF16),
            pltpu.VMEM((3, 2, 2, 16, span), BF16),
            pltpu.VMEM((span, 256), BF16),
            pltpu.VMEM((128, span), BF16),
            pltpu.VMEM((2, 64, 128), F32),
            pltpu.VMEM((3, 32, 256), F32),
            pltpu.VMEM((32, 128), F32),
            pltpu.VMEM((96, 7 * 128), BF16),
            pltpu.VMEM((2, 768, 128), BF16),
            pltpu.VMEM((16, 64), F32),
            pltpu.VMEM((24, 5 * 128), BF16),
            pltpu.VMEM((3, WIN, 128), F32),
            pltpu.VMEM((7 * WIN, 384), BF16),
            pltpu.VMEM((6 * WIN, 384), BF16),
            pltpu.VMEM((WIN, 5 * 128), BF16),
            pltpu.VMEM((24, 256), F32),
            *(pltpu.VMEM((n_date, 8, 128), F32),) * 3,
            pltpu.SemaphoreType.REGULAR,
            dma((5,)),
            dma((2, 2)),
            dma((3, 2)),
            dma((3, 2)),
            dma((3, 2)),
            dma((3, 2)),
            dma((3, n_date)),
            dma((3, n_date)),
        ],
        compiler_params=pltpu.CompilerParams(
            collective_id=0, has_side_effects=True, vmem_limit_bytes=60 * 1024 * 1024
        ),
    )(*operands)


def solution(mesh):
    return jax.shard_map(
        per_device,
        mesh=mesh,
        in_specs=(P(None, "date", "strip", None), P(), P(), P(), P(), P()),
        out_specs=P("date", "strip", None),
        check_vma=False,
    )
```
